256 devices in a mesh: dp: 16 (over y, z_hi, core), ctx: 16 (over z_lo, x).
Axes of the slice: x: 4, y: 4, z: 8 (z_hi: 2, z_lo: 4; z = z_hi * 4 + z_lo), core: 2. Of those that a mesh axis runs over, the one named last changes fastest.
Arguments:
- layer_input: bfloat16 [16, 4096, 8192], P('dp', 'ctx'), may hold values from -6 to 6
- kv_weight: bfloat16 [8192, 256], P('dp'), may hold values from -0.0625 to 0.0625
- kv_stored: bfloat16 [16, 4096, 256], P('dp', 'ctx'), may hold values from -4.5 to 4.5
- queries: bfloat16 [16, 4096, 2048], P('dp', 'ctx'), may hold values from -145 to 145
- grad_out: bfloat16 [16, 4096, 2048], P('dp', 'ctx'), may hold values from -6 to 6
- positions: int32 [4096], P('ctx'), may hold values from 0 to 4095, as said below
Outputs:
- query_grad: bfloat16 [16, 4096, 2048], P('dp', 'ctx')
- input_grad: bfloat16 [16, 4096, 8192], P('dp', 'ctx')
- weight_grad: float32 [8192, 256], P(('dp', 'ctx'))
The draws below stay inside these ranges and needn't reach their ends.
Inputs may be any that keep to these rules, and one draw needn't show every extreme that they name: A permutation of the positions; the 256 slots of index c of ctx hold two blocks of 128 consecutive ascending positions, blocks p and 31 - p of the sequence for some p, in either order.
All inputs are finite; a program needn't handle non-finite values.
Results may differ from the reference program's by a relative error of at most 0.022.
Values may be sent and summed in bfloat16 or wider, within the bound.
No kernel may reach another device: no remote copies, remote signals or barrier semaphores. Data moves between devices by JAX's collectives and lax.ppermute only.
A program may use at most 128 MiB of HBM per device.

```python
import math
import jax
import jax.numpy as jnp
from jax import lax

D = 8192
HEADS = 16
HEAD_DIM = 128
TOK_DEV = 256
BLOCK = 128
SEQ = 4096
BATCH = 16


def shared_keys(key):
    return jnp.clip(jax.random.normal(key, (BATCH, SEQ, HEAD_DIM), jnp.float32), -4.5, 4.5)


def draw_kv_stored(key, part):
    keys_part = shared_keys(key)
    key = jax.random.fold_in(key, 3)
    values = jnp.clip(jax.random.normal(key, (BATCH, SEQ, HEAD_DIM), jnp.float32), -4.5, 4.5)
    return jnp.concatenate([keys_part, values], axis=2).astype(jnp.bfloat16)


def draw_queries(key, part):
    key = jax.random.fold_in(key, 5)
    drawn = jnp.clip(jax.random.normal(key, (BATCH, SEQ, HEADS, HEAD_DIM), jnp.float32), -4.5, 4.5)
    return drawn.reshape(BATCH, SEQ, HEADS * HEAD_DIM).astype(jnp.bfloat16)


def draw_positions(key, part):
    key = jax.random.fold_in(key, 7)
    first_key, second_key = jax.random.split(key)
    pairs = SEQ // TOK_DEV
    order = jax.random.permutation(first_key, pairs)
    flip = jax.random.randint(second_key, (pairs,), 0, 2)
    early = order
    late = 2 * pairs - 1 - order
    leading = jnp.where(flip == 1, late, early)
    trailing = jnp.where(flip == 1, early, late)
    blocks = jnp.stack([leading, trailing], axis=1).reshape(-1)
    slots = blocks[:, None] * BLOCK + jnp.arange(BLOCK)[None, :]
    return slots.reshape(-1).astype(jnp.int32)


def with_spikes(array, own_key, source, target, shards_of, factor):
    owner, partner = [(jnp.arange(array.shape[dim]) // (array.shape[dim] // shards_of)).reshape([-1 if axis == dim else 1 for axis in range(array.ndim)]) for dim in (source, target)]
    chosen = jax.random.permutation(own_key, shards_of)[partner]
    strong = (owner == chosen) | (owner == (partner + shards_of // 2) % shards_of)
    return jnp.where(strong, factor * array, array)


def block_levels(own_key, extent, pieces, least, high):
    level = 1.0
    for dim, parts in pieces:
        steps = jax.random.uniform(jax.random.fold_in(jax.random.fold_in(own_key, 6), dim), (parts,), jnp.float32, least / len(pieces), high / len(pieces))
        level = level * jnp.repeat(jnp.exp(steps), extent[dim] // parts).reshape((-1,) + (1,) * (len(extent) - 1 - dim))
    return level


def normal_values(own_key, shape, spread, bound, shards=(), held_as=jnp.bfloat16):
    entries = spread * jax.random.normal(own_key, shape, jnp.float32)
    if shards:
        entries = entries * block_levels(own_key, shape, shards, -0.22, 0.18)
    return jnp.clip(entries, -bound, bound).astype(held_as)


def gaussian_with(rng, dims, spread, most, cuts, heavy, kind=jnp.bfloat16):
    values = spread * jax.random.normal(rng, dims, jnp.float32)
    if cuts:
        values = values * block_levels(rng, dims, cuts, -0.22, 0.18)
    return jnp.clip(with_spikes(values, jax.random.fold_in(rng, 3), *heavy), -most, most).astype(kind)


def setup_inputs(seed: int = 0) -> dict:
    splits = jax.random.split(jax.random.key(seed), 7)
    return {
        "layer_input": gaussian_with(splits[0], (BATCH, SEQ, D), 1.0, 6.0, ((0, 16), (1, 16)), (1, 2, 16, 2.0)),
        "kv_weight": normal_values(splits[1], (D, 2 * HEAD_DIM), D ** -0.5, 0.0625, ((0, 16),)),
        "kv_stored": draw_kv_stored(jax.random.fold_in(splits[6], 71), 0),
        "queries": draw_queries(jax.random.fold_in(splits[6], 71), 0),
        "grad_out": normal_values(splits[4], (BATCH, SEQ, HEADS * HEAD_DIM), 1.0, 6.0, ((0, 16), (1, 16))),
        "positions": draw_positions(jax.random.fold_in(splits[6], 71), 0),
    }


masked_score = -1e+30

def sequence_grads(query_seq, grad_seq, kv_seq, positions):
    scale = 1.0 / math.sqrt(HEAD_DIM)
    keys = kv_seq[:, :HEAD_DIM].astype(jnp.float32)
    values = kv_seq[:, HEAD_DIM:].astype(jnp.float32)
    query_all = query_seq.reshape(SEQ, HEADS, HEAD_DIM)
    grad_all = grad_seq.reshape(SEQ, HEADS, HEAD_DIM)

    def block_step(carry, block_index):
        key_grad, value_grad = carry
        start = block_index * BLOCK
        query_block = lax.dynamic_slice_in_dim(query_all, start, BLOCK, 0).astype(jnp.float32)
        grad_block = lax.dynamic_slice_in_dim(grad_all, start, BLOCK, 0).astype(jnp.float32)
        query_pos = lax.dynamic_slice_in_dim(positions, start, BLOCK, 0)
        scores = jnp.einsum('thd,kd->thk', query_block, keys) * scale
        visible = positions[None, None, :] <= query_pos[:, None, None]
        top = lax.optimization_barrier(jnp.max(jnp.where(visible, scores, masked_score), axis=-1))
        total = lax.optimization_barrier(jnp.sum(jnp.where(visible, jnp.exp(scores - top[..., None]), 0.0), axis=-1))
        lse = top + jnp.log(total)
        prob = jnp.where(visible, jnp.exp(scores - lse[..., None]), 0.0)
        out = jnp.einsum('thk,kd->thd', prob, values, precision=lax.Precision.HIGHEST)
        dvec = lax.optimization_barrier(jnp.sum(grad_block * out, axis=-1))
        dprob = jnp.einsum('thd,kd->thk', grad_block, values)
        dscore = (prob * (dprob - dvec[..., None]) * scale).astype(jnp.bfloat16)
        prob_low = prob.astype(jnp.bfloat16)
        dscore = lax.optimization_barrier(dscore).astype(jnp.float32)
        prob_low = lax.optimization_barrier(prob_low).astype(jnp.float32)
        query_grad = jnp.einsum('thk,kd->thd', dscore, keys)
        key_grad = key_grad + jnp.einsum('thk,thd->kd', dscore, query_block)
        value_grad = value_grad + jnp.einsum('thk,thd->kd', prob_low, grad_block)
        return ((key_grad, value_grad), query_grad.astype(jnp.bfloat16))
    init = (jnp.zeros((SEQ, HEAD_DIM), jnp.float32), jnp.zeros((SEQ, HEAD_DIM), jnp.float32))
    carry, query_blocks = lax.scan(block_step, init, jnp.arange(SEQ // BLOCK, dtype=jnp.int32))
    kv_grad = jnp.concatenate([carry[0], carry[1]], axis=1)
    return (query_blocks.reshape(SEQ, HEADS * HEAD_DIM), kv_grad)

def reference(layer_input, kv_weight, kv_stored, queries, grad_out, positions):

    def seq_step(total, items):
        input_seq, kv_seq, query_seq, grad_seq = items
        query_grad, kv_grad = sequence_grads(query_seq, grad_seq, kv_seq, positions)
        kv_low = kv_grad.astype(jnp.bfloat16)
        input_grad = jnp.dot(kv_low, kv_weight.T, preferred_element_type=jnp.float32).astype(jnp.bfloat16)
        total = total + jnp.dot(input_seq.T, kv_low, preferred_element_type=jnp.float32)
        return (total, (query_grad, input_grad))
    total, outputs = lax.scan(seq_step, jnp.zeros((D, 2 * HEAD_DIM), jnp.float32), (layer_input, kv_stored, queries, grad_out))
    return (outputs[0], outputs[1], total * (1.0 / math.sqrt(BATCH * SEQ)))
```

```python
import functools
import math

import jax
import jax.numpy as jnp
from jax import lax
from jax.experimental import pallas as pl
from jax.experimental.pallas import tpu as pltpu
from jax.sharding import PartitionSpec as P

BLK = 128
TAG = 16
MASKED = -1e30


def mm(a, b):
    return lax.dot_general(a, b, (((1,), (0,)), ((), ())), preferred_element_type=jnp.float32)


def mm_nt(a, b):
    return lax.dot_general(a, b, (((1,), (1,)), ((), ())), preferred_element_type=jnp.float32)


def attn_kernel(
    G,
    KC,
    blocks,
    scale,
    q_ref,
    do_ref,
    near_ref,
    left_ref,
    right_ref,
    far_a_ref,
    far_b_ref,
    dq_ref,
    keep_ref,
    plus_ref,
    minus_ref,
    plus_late_ref,
    minus_late_ref,
    kvs,
    kT,
    s_scr,
    dp_scr,
    acc,
    dqT,
    qr,
    dor,
    p_even,
    d_even,
    p_odd,
    d_odd,
    first_ref,
):
    R = G * BLK
    c = scale * math.log2(math.e)
    side = pl.program_id(0)
    grp = pl.program_id(1)
    toks = 2 * BLK
    owners = blocks // 2

    @pl.when((side == 0) & (grp == 0))
    def _():
        acc[...] = jnp.zeros_like(acc)
        owner = 0
        for piece in (near_ref, left_ref, right_ref, far_a_ref, far_b_ref):
            for i in range(piece.shape[0] // (toks + TAG)):
                base = i * (toks + TAG)
                mark = piece[base + toks : base + toks + TAG, :BLK].astype(jnp.float32)
                first = jnp.max(mark).astype(jnp.int32)
                first_ref[owner] = first
                for half, place in ((0, first), (1, blocks - 1 - first)):
                    dst = pl.ds(pl.multiple_of(place * BLK, BLK), BLK)
                    blk = piece[base + half * BLK : base + (half + 1) * BLK, :]
                    kvs[dst, :] = blk
                    kT[:, dst] = blk[:, :BLK].T
                owner += 1

    for h in range(G):
        cols = slice(h * BLK, (h + 1) * BLK)
        qr[cols, :] = q_ref[:, cols]
        dor[cols, :] = do_ref[:, cols]
    dqT[...] = jnp.zeros_like(dqT)
    qb = jnp.where(side == 0, first_ref[0], blocks - 1 - first_ref[0])
    nk = (qb + KC // BLK) // (KC // BLK)

    def scores(kc, state, masked):
        m, l, d = state
        rows = pl.ds(pl.multiple_of(kc * KC, KC), KC)
        s = mm_nt(kvs[rows, :BLK], qr[...])
        dp = mm_nt(kvs[rows, BLK:], dor[...])
        if masked:
            kpos = kc * KC + lax.broadcasted_iota(jnp.int32, (KC, R), 0)
            qpos = qb * BLK + (lax.broadcasted_iota(jnp.int32, (KC, R), 1) & (BLK - 1))
            s = jnp.where(kpos <= qpos, s, MASKED)
        s_scr[rows, :] = s
        dp_scr[rows, :] = dp
        s3 = s.reshape(KC // 8, 8, R)
        new = jnp.maximum(m, jnp.max(s3, axis=0))
        p = jnp.exp2((s3 - new[None]) * c)
        f = jnp.exp2((m - new) * c)
        l = l * f + jnp.sum(p, axis=0)
        d = d * f + jnp.sum(p * dp.reshape(KC // 8, 8, R), axis=0)
        return new, l, d

    init = (
        jnp.full((8, R), MASKED, jnp.float32),
        jnp.zeros((8, R), jnp.float32),
        jnp.zeros((8, R), jnp.float32),
    )
    state = lax.fori_loop(0, nk - 1, lambda kc, st: scores(kc, st, False), init)
    m, l, d = scores(nk - 1, state, True)
    top = jnp.max(m, axis=0, keepdims=True)
    f = jnp.exp2((m - top) * c)
    total = jnp.sum(l * f, axis=0, keepdims=True)
    dvec = jnp.sum(d * f, axis=0, keepdims=True) / total
    lse = top * c + jnp.log2(total)

    def weigh(kc, p_buf, d_buf):
        rows = pl.ds(pl.multiple_of(kc * KC, KC), KC)
        p = jnp.exp2(s_scr[rows, :] * c - lse)
        d_buf[...] = (p * (dp_scr[rows, :] - dvec)).astype(jnp.bfloat16)
        p_buf[...] = p.astype(jnp.bfloat16)

    def spend(kc, p_buf, d_buf):
        rows = pl.ds(pl.multiple_of(kc * KC, KC), KC)
        dqT[...] += mm(kT[:, rows], d_buf[...])
        acc[rows, :BLK] += mm(d_buf[...], qr[...])
        acc[rows, BLK:] += mm(p_buf[...], dor[...])

    def pair(t, _):
        kc = 2 * t
        weigh(kc + 1, p_odd, d_odd)
        spend(kc, p_even, d_even)
        weigh(jnp.minimum(kc + 2, nk - 1), p_even, d_even)
        spend(kc + 1, p_odd, d_odd)
        return 0

    weigh(0, p_even, d_even)
    lax.fori_loop(0, nk // 2, pair, 0)

    @pl.when(nk % 2 == 1)
    def _():
        spend(nk - 1, p_even, d_even)

    for h in range(G):
        cols = slice(h * BLK, (h + 1) * BLK)
        dq_ref[:, cols] = (dqT[:, cols].T * scale).astype(jnp.bfloat16)

    @pl.when((side == pl.num_programs(0) - 1) & (grp == pl.num_programs(1) - 1))
    def _():
        span = owners // NX
        cut = span // 2
        for owner in range(owners):
            dx, dz = owner // span, owner % span
            late = dz >= cut
            if dx == 0:
                out, row = keep_ref, dz
            elif dx == 1:
                out, row = (minus_late_ref, dz - cut) if late else (minus_ref, dz)
            elif dx == 2:
                out, row = (plus_ref, dz) if late else (plus_late_ref, dz)
            else:
                out, row = (minus_ref, dz) if late else (plus_ref, dz)
            first = first_ref[owner]
            for half, place in ((0, first), (1, blocks - 1 - first)):
                src = pl.ds(pl.multiple_of(place * BLK, BLK), BLK)
                dst = slice(row * toks + half * BLK, row * toks + (half + 1) * BLK)
                out[dst, :BLK] = (acc[src, :BLK] * scale).astype(jnp.bfloat16)
                out[dst, BLK:] = acc[src, BLK:].astype(jnp.bfloat16)


def attention(q, do, pieces, seq, G=8, KC=256):
    toks, width = q.shape
    heads = width // BLK
    R = G * BLK
    part = pl.BlockSpec((BLK, R), lambda s, g: (s, g))
    quarter = seq // NX

    def whole(rows):
        return pl.BlockSpec((rows, 2 * BLK), lambda s, g: (0, 0), pipeline_mode=pl.Buffered(1))

    out_rows = (quarter, quarter, quarter, quarter // 2, quarter // 2)
    return pl.pallas_call(
        functools.partial(attn_kernel, G, KC, seq // BLK, 1.0 / math.sqrt(BLK)),
        grid=(2, heads // G),
        in_specs=[part, part, *(whole(piece.shape[0]) for piece in pieces)],
        out_specs=[part, *(whole(rows) for rows in out_rows)],
        scratch_shapes=[
            pltpu.VMEM((seq, 2 * BLK), jnp.bfloat16),
            pltpu.VMEM((BLK, seq), jnp.bfloat16),
            pltpu.VMEM((seq, R), jnp.float32),
            pltpu.VMEM((seq, R), jnp.float32),
            pltpu.VMEM((seq, 2 * BLK), jnp.float32),
            pltpu.VMEM((BLK, R), jnp.float32),
            pltpu.VMEM((R, BLK), jnp.bfloat16),
            pltpu.VMEM((R, BLK), jnp.bfloat16),
            *(pltpu.VMEM((KC, R), jnp.bfloat16) for _ in range(4)),
            pltpu.SMEM((seq // BLK // 2,), jnp.int32),
        ],
        out_shape=[
            jax.ShapeDtypeStruct((toks, width), jnp.bfloat16),
            *(jax.ShapeDtypeStruct((rows, 2 * BLK), jnp.bfloat16) for rows in out_rows),
        ],
        compiler_params=pltpu.CompilerParams(
            dimension_semantics=("arbitrary", "arbitrary"), vmem_limit_bytes=60 * 2**20
        ),
        cost_estimate=pl.CostEstimate(
            flops=40 * 10**9, bytes_accessed=8 * 2**20, transcendentals=2 * 10**7
        ),
    )(q, do, *pieces)


NZ, NX = 4, 4
NY, NH, NC = 4, 2, 2
CORE_PAIRS = [(i, i ^ 1) for i in range(NY * NH * NC)]
FAR_PAIRS = [(i, i ^ NC) for i in range(NY * NH * NC)]


def along_x(array, step):
    pairs = [
        (z * NX + x, z * NX + (x + step) % NX) for z in range(NZ) for x in range(NX)
    ]
    return lax.ppermute(array, "ctx", pairs)


def along_z(array, step):
    pairs = [
        (z * NX + x, (z + step) % NZ * NX + x) for z in range(NZ) for x in range(NX)
    ]
    return lax.ppermute(array, "ctx", pairs)


def along_y(array, step):
    rest = NH * NC
    pairs = [(i, (i + step * rest) % (NY * rest)) for i in range(NY * rest)]
    return lax.ppermute(array, "dp", pairs)


def cut_kernel(core_ref, a_ref, b_ref, mine_ref, theirs_ref):
    mine_ref[0] = a_ref[...].T
    theirs_ref[0] = b_ref[...].T


def cut_features(features, core):
    toks, model = features.shape
    piece = model // (NY * NH * NC)
    out = jax.ShapeDtypeStruct((NY * NH, piece, toks), features.dtype)
    gs = pltpu.PrefetchScalarGridSpec(
        num_scalar_prefetch=1,
        grid=(NY * NH,),
        in_specs=[
            pl.BlockSpec((toks, piece), lambda i, core: (0, NC * i + core[0])),
            pl.BlockSpec((toks, piece), lambda i, core: (0, NC * i + 1 - core[0])),
        ],
        out_specs=[pl.BlockSpec((1, piece, toks), lambda i, core: (i, 0, 0))] * 2,
    )
    return pl.pallas_call(
        cut_kernel,
        grid_spec=gs,
        out_shape=[out, out],
        cost_estimate=pl.CostEstimate(flops=0, bytes_accessed=8 * 2**20, transcendentals=0),
    )(core.reshape(1), features, features)


def project_kernel(factor, at_ref, mine_ref, theirs_ref, grad_ref, other_ref, out_ref):
    total = mm(mine_ref[0], grad_ref[...]) + mm(theirs_ref[0], other_ref[...])
    total = (total * factor).astype(out_ref.dtype)
    rows = total.shape[0] // (NZ * NX)
    for z in range(NZ):
        dz = (z + NZ - at_ref[0]) % NZ
        for x in range(NX):
            dx = (x + NX - at_ref[1]) % NX
            src = (z * NX + x) * rows
            to = pl.multiple_of((dx * NZ + dz) * rows, rows)
            out_ref[0, pl.ds(to, rows), :] = total[src : src + rows, :]


def project(mine, theirs, grad, other, at, start, count, factor):
    _, piece, toks = mine.shape
    width = grad.shape[1]
    features = pl.BlockSpec((1, piece, toks), lambda i, at: (at[2 + start + i], 0, 0))
    gs = pltpu.PrefetchScalarGridSpec(
        num_scalar_prefetch=1,
        grid=(count,),
        in_specs=[
            features,
            features,
            pl.BlockSpec((toks, width), lambda i, at: (0, 0)),
            pl.BlockSpec((toks, width), lambda i, at: (0, 0)),
        ],
        out_specs=pl.BlockSpec((1, piece, width), lambda i, at: (i, 0, 0)),
    )
    return pl.pallas_call(
        functools.partial(project_kernel, factor),
        grid_spec=gs,
        out_shape=jax.ShapeDtypeStruct((count, piece, width), jnp.bfloat16),
        cost_estimate=pl.CostEstimate(
            flops=2**28 * count, bytes_accessed=2**20 * count, transcendentals=0
        ),
    )(at, mine, theirs, grad, other)


def total_of(*parts):
    return sum(part.astype(jnp.float32) for part in parts)


def body(layer_input, kv_weight, kv_stored, queries, grad_out, positions):
    low = jnp.bfloat16
    tok_rows = queries.shape[1]
    width = kv_weight.shape[1]
    ctx_size = lax.axis_size("ctx")
    data_size = lax.axis_size("dp")
    seq_rows = tok_rows * ctx_size
    data_at, ctx_at = lax.axis_index("dp"), lax.axis_index("ctx")
    y_at, far_at, core_at = data_at // (NH * NC), data_at // NC % NH, data_at % NC
    z_at, x_at = ctx_at // NX, ctx_at % NX

    tag = jnp.full((TAG, width), (positions[0] // BLK).astype(low), low)
    tagged = jnp.concatenate([kv_stored[0], tag], axis=0)
    near = jnp.concatenate([tagged, *(along_z(tagged, step) for step in range(1, NZ))], axis=0)
    half = near.shape[0] // 2
    left, right = along_x(near, 1), along_x(near, -1)
    far_a, far_b = along_x(left[:half], 1), along_x(right[half:], -1)

    mine, theirs = cut_features(layer_input[0], core_at)
    query, mine, theirs = lax.optimization_barrier((queries[0], mine, theirs))
    theirs = lax.ppermute(theirs, "dp", CORE_PAIRS)

    query_grad, keep, plus, minus, plus_late, minus_late = attention(
        query, grad_out[0], (near, left, right, far_a, far_b), seq_rows
    )
    weight = lax.all_gather(kv_weight, "dp", axis=0, tiled=True)

    cut = plus_late.shape[0]
    from_left, from_right = along_x(plus, 1), along_x(minus, -1)
    plus_late = total_of(plus_late, from_left[:cut]).astype(low)
    minus_late = total_of(minus_late, from_right[cut:]).astype(low)
    late_left, late_right = along_x(plus_late, 1), along_x(minus_late, -1)
    early = total_of(keep[:cut], late_left, from_right[:cut]).astype(low)
    late = total_of(keep[cut:], from_left[cut:], late_right).astype(low)
    spans = [early[:tok_rows], early[tok_rows:], late[:tok_rows], late[tok_rows:]]
    spans = [spans[0], *(along_z(spans[step], -step) for step in range(1, NZ))]
    owned = total_of(*spans).astype(low)

    other = lax.ppermute(owned, "dp", CORE_PAIRS)

    steps = ((2, 0), (1, 1), (3, 0), (2, 1), (1, 0), (3, 1), (0, 0), (0, 1))
    chunks = [(y_at + dy) % NY * NH + (far_at + dh) % NH for dy, dh in steps]
    at = jnp.stack([z_at, x_at, *chunks]).astype(jnp.int32)

    def terms_for(start, count):
        factor = 1.0 / math.sqrt(data_size * seq_rows)
        return project(mine, theirs, owned, other, at, start, count, factor)

    from_plus = along_y(terms_for(0, 2), 1)
    from_minus = along_y(terms_for(2, 2), -1)
    rest = terms_for(4, 4)
    late_plus = along_y(total_of(rest[0], from_plus[0]).astype(low), 1)
    late_minus = along_y(total_of(rest[1], from_minus[1]).astype(low), -1)
    input_grad = lax.dot_general(
        owned, weight, (((1,), (1,)), ((), ())), preferred_element_type=jnp.float32
    ).astype(low)[None]
    late_plus, late_minus, input_grad = lax.optimization_barrier(
        (late_plus, late_minus, input_grad)
    )
    halves = (
        total_of(rest[2], late_plus, from_minus[0]).astype(low),
        total_of(rest[3], from_plus[1], late_minus).astype(low),
    )
    terms = jnp.stack([half.reshape(NX, -1, width) for half in halves], axis=1)
    terms = terms.reshape(NX, -1, width)
    terms = total_of(terms[0], *(along_x(terms[step], step) for step in range(1, NX))).astype(low)
    terms = terms.reshape(NH, NZ, -1, width)
    terms = total_of(terms[:, 0], *(along_z(terms[:, step], step) for step in range(1, NZ)))
    weight_grad = terms[0] + lax.ppermute(terms[1], "dp", FAR_PAIRS)

    return (query_grad[None], input_grad, weight_grad)


def solution(mesh):
    placed = (
        P("dp", "ctx", None),
        P("dp", None),
        P("dp", "ctx", None),
        P("dp", "ctx", None),
        P("dp", "ctx", None),
        P("ctx"),
    )
    return jax.shard_map(
        body,
        mesh=mesh,
        in_specs=placed,
        out_specs=(P("dp", "ctx", None), P("dp", "ctx", None), P(("dp", "ctx"), None)),
        check_vma=False,
    )
```

```python
import functools
import math

import jax
import jax.numpy as jnp
from jax import lax
from jax.experimental import pallas as pl
from jax.experimental.pallas import tpu as pltpu
from jax.sharding import PartitionSpec as P

BLK = 128
TAG = 16
MASKED = -1e30
LONG = 4


def mm(a, b):
    return lax.dot_general(a, b, (((1,), (0,)), ((), ())), preferred_element_type=jnp.float32)


def mm_tn(a, b):
    return lax.dot_general(a, b, (((0,), (0,)), ((), ())), preferred_element_type=jnp.float32)


def mm_nt(a, b):
    return lax.dot_general(a, b, (((1,), (1,)), ((), ())), preferred_element_type=jnp.float32)


def attn_kernel(
    G,
    KC,
    blocks,
    scale,
    q_ref,
    do_ref,
    near_ref,
    left_ref,
    right_ref,
    far_a_ref,
    far_b_ref,
    dq_ref,
    keep_ref,
    plus_ref,
    minus_ref,
    plus_late_ref,
    minus_late_ref,
    kvs,
    s_scr,
    dp_scr,
    acc,
    dq_acc,
    qr,
    dor,
    p_even,
    d_even,
    p_odd,
    d_odd,
    first_ref,
):
    R = G * BLK
    c = scale * math.log2(math.e)
    side = pl.program_id(0)
    grp = pl.program_id(1)
    toks = 2 * BLK
    owners = blocks // 2

    @pl.when((side == 0) & (grp == 0))
    def _():
        acc[...] = jnp.zeros_like(acc)
        owner = 0
        for piece in (near_ref, left_ref, right_ref, far_a_ref, far_b_ref):
            for i in range(piece.shape[0] // (toks + TAG)):
                base = i * (toks + TAG)
                mark = piece[base + toks : base + toks + TAG, :BLK].astype(jnp.float32)
                first = jnp.max(mark).astype(jnp.int32)
                first_ref[owner] = first
                for half, place in ((0, first), (1, blocks - 1 - first)):
                    dst = pl.ds(pl.multiple_of(place * BLK, BLK), BLK)
                    kvs[dst, :] = piece[base + half * BLK : base + (half + 1) * BLK, :]
                owner += 1

    for h in range(G):
        cols = slice(h * BLK, (h + 1) * BLK)
        qr[cols, :] = q_ref[:, cols]
        dor[cols, :] = do_ref[:, cols]
    dq_acc[...] = jnp.zeros_like(dq_acc)
    qb = jnp.where(side == 0, first_ref[0], blocks - 1 - first_ref[0])
    nk = (qb + KC // BLK) // (KC // BLK)

    def scores(start, size, state, masked):
        m, l, d = state
        rows = pl.ds(pl.multiple_of(start, KC), size)
        s = mm_nt(kvs[rows, :BLK], qr[...])
        dp = mm_nt(kvs[rows, BLK:], dor[...])
        if masked:
            kpos = start + lax.broadcasted_iota(jnp.int32, (size, R), 0)
            qpos = qb * BLK + (lax.broadcasted_iota(jnp.int32, (size, R), 1) & (BLK - 1))
            s = jnp.where(kpos <= qpos, s, MASKED)
        s_scr[rows, :] = s
        dp_scr[rows, :] = dp
        s3 = s.reshape(size // 8, 8, R)
        new = jnp.maximum(m, jnp.max(s3, axis=0))
        p = jnp.exp2((s3 - new[None]) * c)
        f = jnp.exp2((m - new) * c)
        l = l * f + jnp.sum(p, axis=0)
        d = d * f + jnp.sum(p * dp.reshape(size // 8, 8, R), axis=0)
        return new, l, d

    state = (
        jnp.full((8, R), MASKED, jnp.float32),
        jnp.zeros((8, R), jnp.float32),
        jnp.zeros((8, R), jnp.float32),
    )
    runs = (nk - 1) // LONG
    state = lax.fori_loop(
        0, runs, lambda i, state: scores(i * LONG * KC, LONG * KC, state, False), state
    )
    state = lax.fori_loop(
        runs * LONG, nk - 1, lambda i, state: scores(i * KC, KC, state, False), state
    )
    m, l, d = scores((nk - 1) * KC, KC, state, True)
    top = jnp.max(m, axis=0, keepdims=True)
    f = jnp.exp2((m - top) * c)
    total = jnp.sum(l * f, axis=0, keepdims=True)
    dvec = jnp.sum(d * f, axis=0, keepdims=True) / total
    lse = top * c + jnp.log2(total)

    def weigh(start, size, p_buf, d_buf):
        rows = pl.ds(pl.multiple_of(start, KC), size)
        p = jnp.exp2(s_scr[rows, :] * c - lse)
        d_buf[:size, :] = (p * (dp_scr[rows, :] - dvec)).astype(jnp.bfloat16)
        p_buf[:size, :] = p.astype(jnp.bfloat16)

    def spend(start, size, p_buf, d_buf):
        rows = pl.ds(pl.multiple_of(start, KC), size)
        dq_acc[...] += mm_tn(d_buf[:size, :], kvs[rows, :BLK])
        acc[rows, :BLK] += mm(d_buf[:size, :], qr[...])
        acc[rows, BLK:] += mm(p_buf[:size, :], dor[...])

    run = p_even.shape[0]
    pairs = nk // (2 * run // KC)

    @pl.when(pairs > 0)
    def _():
        weigh(0, run, p_even, d_even)

    def pair(i, _):
        start = i * 2 * run
        weigh(start + run, run, p_odd, d_odd)
        spend(start, run, p_even, d_even)
        weigh(jnp.minimum(start + 2 * run, blocks * BLK - run), run, p_even, d_even)
        spend(start + run, run, p_odd, d_odd)
        return 0

    def single(i, _):
        weigh(i * KC, KC, p_even, d_even)
        spend(i * KC, KC, p_even, d_even)
        return 0

    lax.fori_loop(0, pairs, pair, 0)
    lax.fori_loop(pairs * (2 * run // KC), nk, single, 0)

    for h in range(G):
        cols = slice(h * BLK, (h + 1) * BLK)
        dq_ref[:, cols] = (dq_acc[cols, :] * scale).astype(jnp.bfloat16)

    @pl.when((side == pl.num_programs(0) - 1) & (grp == pl.num_programs(1) - 1))
    def _():
        span = owners // NX
        cut = span // 2
        for owner in range(owners):
            dx, dz = owner // span, owner % span
            late = dz >= cut
            if dx == 0:
                out, row = keep_ref, dz
            elif dx == 1:
                out, row = (minus_late_ref, dz - cut) if late else (minus_ref, dz)
            elif dx == 2:
                out, row = (plus_ref, dz) if late else (plus_late_ref, dz)
            else:
                out, row = (minus_ref, dz) if late else (plus_ref, dz)
            first = first_ref[owner]
            for half, place in ((0, first), (1, blocks - 1 - first)):
                src = pl.ds(pl.multiple_of(place * BLK, BLK), BLK)
                dst = slice(row * toks + half * BLK, row * toks + (half + 1) * BLK)
                out[dst, :BLK] = (acc[src, :BLK] * scale).astype(jnp.bfloat16)
                out[dst, BLK:] = acc[src, BLK:].astype(jnp.bfloat16)


def attention(q, do, pieces, seq, G=8, KC=256):
    toks, width = q.shape
    heads = width // BLK
    R = G * BLK
    part = pl.BlockSpec((BLK, R), lambda s, g: (s, g))
    quarter = seq // NX

    def whole(rows):
        return pl.BlockSpec((rows, 2 * BLK), lambda s, g: (0, 0), pipeline_mode=pl.Buffered(1))

    out_rows = (quarter, quarter, quarter, quarter // 2, quarter // 2)
    return pl.pallas_call(
        functools.partial(attn_kernel, G, KC, seq // BLK, 1.0 / math.sqrt(BLK)),
        grid=(2, heads // G),
        in_specs=[part, part, *(whole(piece.shape[0]) for piece in pieces)],
        out_specs=[part, *(whole(rows) for rows in out_rows)],
        scratch_shapes=[
            pltpu.VMEM((seq, 2 * BLK), jnp.bfloat16),
            pltpu.VMEM((seq, R), jnp.float32),
            pltpu.VMEM((seq, R), jnp.float32),
            pltpu.VMEM((seq, 2 * BLK), jnp.float32),
            pltpu.VMEM((R, BLK), jnp.float32),
            pltpu.VMEM((R, BLK), jnp.bfloat16),
            pltpu.VMEM((R, BLK), jnp.bfloat16),
            *(pltpu.VMEM((LONG // 2 * KC, R), jnp.bfloat16) for _ in range(4)),
            pltpu.SMEM((seq // BLK // 2,), jnp.int32),
        ],
        out_shape=[
            jax.ShapeDtypeStruct((toks, width), jnp.bfloat16),
            *(jax.ShapeDtypeStruct((rows, 2 * BLK), jnp.bfloat16) for rows in out_rows),
        ],
        compiler_params=pltpu.CompilerParams(
            dimension_semantics=("arbitrary", "arbitrary"), vmem_limit_bytes=60 * 2**20
        ),
        cost_estimate=pl.CostEstimate(
            flops=40 * 10**9, bytes_accessed=8 * 2**20, transcendentals=2 * 10**7
        ),
    )(q, do, *pieces)


NZ, NX = 4, 4
NY, NH, NC = 4, 2, 2
CORE_PAIRS = [(i, i ^ 1) for i in range(NY * NH * NC)]


def along_x(array, step):
    pairs = [
        (z * NX + x, z * NX + (x + step) % NX) for z in range(NZ) for x in range(NX)
    ]
    return lax.ppermute(array, "ctx", pairs)


def along_z(array, step):
    pairs = [
        (z * NX + x, (z + step) % NZ * NX + x) for z in range(NZ) for x in range(NX)
    ]
    return lax.ppermute(array, "ctx", pairs)


def swap_x(array, bits):
    pairs = [(i, i ^ bits) for i in range(NZ * NX)]
    return lax.ppermute(array, "ctx", pairs)


def swap_z(array, bits):
    high, low_bits = bits // NZ, bits % NZ
    size = NZ * NX
    pairs = [
        (i * size + j, (i ^ high * NC) * size + (j ^ low_bits * NX))
        for i in range(NY * NH * NC)
        for j in range(size)
    ]
    return lax.ppermute(array, ("dp", "ctx"), pairs)


X_SWAPS = (1, 3)
Z_SWAPS = (1, 3, 7)


def swap_order(swaps):
    order = [0]
    for bits in reversed(swaps):
        order += [place ^ bits for place in order]
    return order


def along_y(array, step):
    rest = NH * NC
    pairs = [(i, (i + step * rest) % (NY * rest)) for i in range(NY * rest)]
    return lax.ppermute(array, "dp", pairs)


def tag_kernel(positions_ref, kv_ref, out_ref):
    toks = kv_ref.shape[0]
    out_ref[:toks, :] = kv_ref[...]
    first = (positions_ref[0] // BLK).astype(jnp.float32)
    out_ref[toks:, :] = jnp.full((TAG, kv_ref.shape[1]), first).astype(out_ref.dtype)


def tagged_tokens(positions, kv):
    toks, width = kv.shape
    return pl.pallas_call(
        tag_kernel,
        in_specs=[
            pl.BlockSpec(memory_space=pltpu.SMEM),
            pl.BlockSpec(memory_space=pltpu.VMEM),
        ],
        out_specs=pl.BlockSpec(memory_space=pltpu.VMEM),
        out_shape=jax.ShapeDtypeStruct((toks + TAG, width), kv.dtype),
    )(positions, kv)


def cut_kernel(at_ref, a_ref, out_ref):
    out_ref[...] = a_ref[...].T


def cut_features(features, at, start, count):
    toks, model = features.shape
    piece = model // (NY * NH)
    gs = pltpu.PrefetchScalarGridSpec(
        num_scalar_prefetch=1,
        grid=(count,),
        in_specs=[pl.BlockSpec((toks, piece), lambda i, at: (0, at[start + i]))],
        out_specs=pl.BlockSpec((piece, toks), lambda i, at: (i, 0)),
    )
    return pl.pallas_call(
        cut_kernel,
        grid_spec=gs,
        out_shape=jax.ShapeDtypeStruct((count * piece, toks), features.dtype),
        cost_estimate=pl.CostEstimate(
            flops=0, bytes_accessed=2**20 * count, transcendentals=0
        ),
    )(at, features)


def project_kernel(factor, at_ref, a_ref, b_ref, c_ref, d0_ref, d1_ref, g0, g1, g2, g3, out_ref):
    h = pl.program_id(0)
    far = jnp.where(h == 0, d0_ref[...], d1_ref[...])
    total = mm(a_ref[...], g0[...]) + mm(b_ref[...], g1[...])
    total = total + mm(c_ref[...], g2[...]) + mm(far, g3[...])
    total = (total * factor).astype(out_ref.dtype)
    rows = total.shape[0] // (NZ * NX)
    x_order, z_order = swap_order(X_SWAPS), swap_order(Z_SWAPS)
    x_rank = [0] * len(x_order)
    for rank, place in enumerate(x_order):
        x_rank[place] = rank
    z_rank = [0] * len(z_order)
    for rank, place in enumerate(z_order):
        z_rank[place] = rank

    def ranked(ranks, place):
        found = jnp.int32(0)
        for i, rank in enumerate(ranks):
            found = jnp.where(place == i, rank, found)
        return found

    x_to = [ranked(x_rank, x ^ at_ref[1]) for x in range(NX)]
    for z in range(NZ):
        z_to = ranked(z_rank, (h * NZ + z) ^ at_ref[0])
        for x in range(NX):
            src = (z * NX + x) * rows
            to = pl.multiple_of((x_to[x] * NH * NZ + z_to) * rows, rows)
            out_ref[pl.ds(to, rows), :] = total[src : src + rows, :]


def project(home, left, right, far_a, far_b, grads, at, which, factor):
    toks, width = grads[0].shape
    piece = home.shape[0] // (NH * NC)
    full = pl.BlockSpec((piece, toks), lambda i, at: (i * NC + at[2 + which], 0))
    half = pl.BlockSpec((piece, toks), lambda i, at: (at[2 + which], 0))
    grad = pl.BlockSpec((toks, width), lambda i, at: (0, 0))
    gs = pltpu.PrefetchScalarGridSpec(
        num_scalar_prefetch=1,
        grid=(NH,),
        in_specs=[full, full, full, half, half] + [grad] * 4,
        out_specs=pl.BlockSpec((NH * piece, width), lambda i, at: (0, 0)),
    )
    return pl.pallas_call(
        functools.partial(project_kernel, factor),
        grid_spec=gs,
        out_shape=jax.ShapeDtypeStruct((NH * piece, width), jnp.bfloat16),
        cost_estimate=pl.CostEstimate(
            flops=2**30, bytes_accessed=3 * 2**20, transcendentals=0
        ),
    )(at, home, left, right, far_a, far_b, *grads)


def total_of(*parts):
    return sum(part.astype(jnp.float32) for part in parts)


def project_back(grads, weight):
    return lax.dot_general(
        grads, weight, (((1,), (1,)), ((), ())), preferred_element_type=jnp.float32
    ).astype(jnp.bfloat16)[None]


def body(layer_input, kv_weight, kv_stored, queries, grad_out, positions):
    low = jnp.bfloat16
    tok_rows = queries.shape[1]
    width = kv_weight.shape[1]
    ctx_size = lax.axis_size("ctx")
    data_size = lax.axis_size("dp")
    seq_rows = tok_rows * ctx_size
    data_at, ctx_at = lax.axis_index("dp"), lax.axis_index("ctx")
    y_at, far_at, core_at = data_at // (NH * NC), data_at // NC % NH, data_at % NC
    z_at, x_at = ctx_at // NX, ctx_at % NX

    tagged = tagged_tokens(positions, kv_stored[0])
    steps = ((1, 0), (1, 1), (2, 0), (3, 0), (3, 1), (2, 1), (0, 0), (0, 1))
    table = [(y_at + dy) % NY * NH + h for dy, h in steps]
    at = jnp.stack([far_at * NZ + z_at, x_at, 1 - core_at, core_at, *table]).astype(jnp.int32)
    plus = cut_features(layer_input[0], at, 4, 3)
    minus = cut_features(layer_input[0], at, 7, 3)
    home = cut_features(layer_input[0], at, 10, 2)

    column = [along_z(tagged, step) for step in range(1, NZ)]
    *column, plus = lax.optimization_barrier((*column, plus))
    near = jnp.concatenate([tagged, *column], axis=0)
    half = near.shape[0] // 2
    left, right = along_x(near, 1), along_x(near, -1)
    left, right, minus, home = lax.optimization_barrier((left, right, minus, home))
    far_a, far_b = along_x(left[:half], 1), along_x(right[half:], -1)

    query, plus, minus = lax.optimization_barrier((queries[0], plus, minus))
    from_left, from_right = along_y(plus, 1), along_y(minus, -1)

    query_grad, *sums = attention(
        query, grad_out[0], (near, left, right, far_a, far_b), seq_rows
    )
    from_left, from_right, *sums = lax.optimization_barrier((from_left, from_right, *sums))
    keep, plus, minus, plus_late, minus_late = sums
    full = home.shape[0]
    weight = lax.all_gather(kv_weight, "dp", axis=0, tiled=True)

    cut = plus_late.shape[0]
    feats_left, feats_right = from_left, from_right
    from_left, from_right = along_x(plus, 1), along_x(minus, -1)
    from_left, from_right, feats_a, feats_b = lax.optimization_barrier(
        (from_left, from_right, feats_left[full:], feats_right[full:])
    )
    feats_a, feats_b = along_y(feats_a, 1), along_y(feats_b, -1)
    plus_late = total_of(plus_late, from_left[:cut]).astype(low)
    minus_late = total_of(minus_late, from_right[cut:]).astype(low)
    late_left, late_right = along_x(plus_late, 1), along_x(minus_late, -1)
    late_left, late_right, feats_a, feats_b = lax.optimization_barrier(
        (late_left, late_right, feats_a, feats_b)
    )
    early = total_of(keep[:cut], late_left, from_right[:cut]).astype(low)
    late = total_of(keep[cut:], from_left[cut:], late_right).astype(low)
    spans = [early[:tok_rows], early[tok_rows:], late[:tok_rows], late[tok_rows:]]
    spans = [spans[0], *(along_z(spans[step], -step) for step in range(1, NZ))]
    owned = total_of(*spans).astype(low)

    grads = [along_y(owned, 1), along_y(owned, -1), along_y(owned, 2)]

    def terms_for(which):
        factor = 1.0 / math.sqrt(data_size * seq_rows)
        feats = (home, feats_left, feats_right, feats_a, feats_b)
        return project(*feats, (owned, *grads), at, which, factor)

    other = lax.ppermute(terms_for(0), "dp", CORE_PAIRS)
    terms, input_grad = total_of(terms_for(1), other), None
    for swap, swaps in ((swap_x, X_SWAPS), (swap_z, Z_SWAPS)):
        for bits in swaps:
            terms = terms.astype(low)
            cut = terms.shape[0] // 2
            came = swap(terms[cut:], bits)
            if input_grad is None:
                input_grad = project_back(owned, weight)
                came, input_grad = lax.optimization_barrier((came, input_grad))
            terms = total_of(terms[:cut], came)
    weight_grad = terms

    return (query_grad[None], input_grad, weight_grad)


def solution(mesh):
    placed = (
        P("dp", "ctx", None),
        P("dp", None),
        P("dp", "ctx", None),
        P("dp", "ctx", None),
        P("dp", "ctx", None),
        P("ctx"),
    )
    return jax.shard_map(
        body,
        mesh=mesh,
        in_specs=placed,
        out_specs=(P("dp", "ctx", None), P("dp", "ctx", None), P(("dp", "ctx"), None)),
        check_vma=False,
    )
```

```python
import functools
import math

import jax
import jax.numpy as jnp
from jax import lax
from jax.experimental import pallas as pl
from jax.experimental.pallas import tpu as pltpu
from jax.sharding import PartitionSpec as P

BLK = 128
TAG = 16
MASKED = -1e30
LONG = 4


def mm(a, b):
    return lax.dot_general(a, b, (((1,), (0,)), ((), ())), preferred_element_type=jnp.float32)


def mm_tn(a, b):
    return lax.dot_general(a, b, (((0,), (0,)), ((), ())), preferred_element_type=jnp.float32)


def mm_nt(a, b):
    return lax.dot_general(a, b, (((1,), (1,)), ((), ())), preferred_element_type=jnp.float32)


def attn_kernel(
    G,
    KC,
    blocks,
    scale,
    q_ref,
    do_ref,
    near_ref,
    left_ref,
    right_ref,
    far_a_ref,
    far_b_ref,
    dq_ref,
    keep_ref,
    plus_ref,
    minus_ref,
    plus_late_ref,
    minus_late_ref,
    kvs,
    s_scr,
    dp_scr,
    acc,
    dq_acc,
    qr,
    dor,
    p_even,
    d_even,
    p_odd,
    d_odd,
    first_ref,
):
    R = G * BLK
    c = scale * math.log2(math.e)
    side = pl.program_id(0)
    grp = pl.program_id(1)
    toks = 2 * BLK
    owners = blocks // 2

    @pl.when((side == 0) & (grp == 0))
    def _():
        acc[...] = jnp.zeros_like(acc)
        owner = 0
        for piece in (near_ref, left_ref, right_ref, far_a_ref, far_b_ref):
            for i in range(piece.shape[0] // (toks + TAG)):
                base = i * (toks + TAG)
                mark = piece[base + toks : base + toks + TAG, :BLK].astype(jnp.float32)
                first = jnp.max(mark).astype(jnp.int32)
                first_ref[owner] = first
                for half, place in ((0, first), (1, blocks - 1 - first)):
                    dst = pl.ds(pl.multiple_of(place * BLK, BLK), BLK)
                    kvs[dst, :] = piece[base + half * BLK : base + (half + 1) * BLK, :]
                owner += 1

    for h in range(G):
        cols = slice(h * BLK, (h + 1) * BLK)
        qr[cols, :] = q_ref[:, cols]
        dor[cols, :] = do_ref[:, cols]
    dq_acc[...] = jnp.zeros_like(dq_acc)
    qb = jnp.where(side == 0, first_ref[0], blocks - 1 - first_ref[0])
    nk = (qb + KC // BLK) // (KC // BLK)

    def scores(start, size, state, masked):
        m, l, d = state
        rows = pl.ds(pl.multiple_of(start, KC), size)
        s = mm_nt(kvs[rows, :BLK], qr[...])
        dp = mm_nt(kvs[rows, BLK:], dor[...])
        if masked:
            kpos = start + lax.broadcasted_iota(jnp.int32, (size, R), 0)
            qpos = qb * BLK + (lax.broadcasted_iota(jnp.int32, (size, R), 1) & (BLK - 1))
            s = jnp.where(kpos <= qpos, s, MASKED)
        s_scr[rows, :] = s
        dp_scr[rows, :] = dp
        s3 = s.reshape(size // 8, 8, R)
        new = jnp.maximum(m, jnp.max(s3, axis=0))
        p = jnp.exp2((s3 - new[None]) * c)
        f = jnp.exp2((m - new) * c)
        l = l * f + jnp.sum(p, axis=0)
        d = d * f + jnp.sum(p * dp.reshape(size // 8, 8, R), axis=0)
        return new, l, d

    state = (
        jnp.full((8, R), MASKED, jnp.float32),
        jnp.zeros((8, R), jnp.float32),
        jnp.zeros((8, R), jnp.float32),
    )
    runs = (nk - 1) // LONG
    state = lax.fori_loop(
        0, runs, lambda i, state: scores(i * LONG * KC, LONG * KC, state, False), state
    )
    state = lax.fori_loop(
        runs * LONG, nk - 1, lambda i, state: scores(i * KC, KC, state, False), state
    )
    m, l, d = scores((nk - 1) * KC, KC, state, True)
    top = jnp.max(m, axis=0, keepdims=True)
    f = jnp.exp2((m - top) * c)
    total = jnp.sum(l * f, axis=0, keepdims=True)
    dvec = jnp.sum(d * f, axis=0, keepdims=True) / total
    lse = top * c + jnp.log2(total)

    def weigh(start, size, p_buf, d_buf):
        rows = pl.ds(pl.multiple_of(start, KC), size)
        p = jnp.exp2(s_scr[rows, :] * c - lse)
        d_buf[:size, :] = (p * (dp_scr[rows, :] - dvec)).astype(jnp.bfloat16)
        p_buf[:size, :] = p.astype(jnp.bfloat16)

    def spend(start, size, p_buf, d_buf):
        rows = pl.ds(pl.multiple_of(start, KC), size)
        dq_acc[...] += mm_tn(d_buf[:size, :], kvs[rows, :BLK])
        acc[rows, :BLK] += mm(d_buf[:size, :], qr[...])
        acc[rows, BLK:] += mm(p_buf[:size, :], dor[...])

    run = p_even.shape[0]
    pairs = nk // (2 * run // KC)

    @pl.when(pairs > 0)
    def _():
        weigh(0, run, p_even, d_even)

    def pair(i, _):
        start = i * 2 * run
        weigh(start + run, run, p_odd, d_odd)
        spend(start, run, p_even, d_even)
        weigh(jnp.minimum(start + 2 * run, blocks * BLK - run), run, p_even, d_even)
        spend(start + run, run, p_odd, d_odd)
        return 0

    def single(i, _):
        weigh(i * KC, KC, p_even, d_even)
        spend(i * KC, KC, p_even, d_even)
        return 0

    lax.fori_loop(0, pairs, pair, 0)
    lax.fori_loop(pairs * (2 * run // KC), nk, single, 0)

    for h in range(G):
        cols = slice(h * BLK, (h + 1) * BLK)
        dq_ref[:, cols] = (dq_acc[cols, :] * scale).astype(jnp.bfloat16)

    @pl.when((side == pl.num_programs(0) - 1) & (grp == pl.num_programs(1) - 1))
    def _():
        span = owners // NX
        cut = span // 2
        for owner in range(owners):
            dx, dz = owner // span, owner % span
            late = dz >= cut
            if dx == 0:
                out, row = keep_ref, dz
            elif dx == 1:
                out, row = (minus_late_ref, dz - cut) if late else (minus_ref, dz)
            elif dx == 2:
                out, row = (plus_ref, dz) if late else (plus_late_ref, dz)
            else:
                out, row = (minus_ref, dz) if late else (plus_ref, dz)
            first = first_ref[owner]
            for half, place in ((0, first), (1, blocks - 1 - first)):
                src = pl.ds(pl.multiple_of(place * BLK, BLK), BLK)
                dst = slice(row * toks + half * BLK, row * toks + (half + 1) * BLK)
                out[dst, :BLK] = (acc[src, :BLK] * scale).astype(jnp.bfloat16)
                out[dst, BLK:] = acc[src, BLK:].astype(jnp.bfloat16)


def attention(q, do, pieces, seq, G=8, KC=256):
    toks, width = q.shape
    heads = width // BLK
    R = G * BLK
    part = pl.BlockSpec((BLK, R), lambda s, g: (s, g))
    quarter = seq // NX

    def whole(rows):
        return pl.BlockSpec((rows, 2 * BLK), lambda s, g: (0, 0), pipeline_mode=pl.Buffered(1))

    out_rows = (quarter, quarter, quarter, quarter // 2, quarter // 2)
    return pl.pallas_call(
        functools.partial(attn_kernel, G, KC, seq // BLK, 1.0 / math.sqrt(BLK)),
        grid=(2, heads // G),
        in_specs=[part, part, *(whole(piece.shape[0]) for piece in pieces)],
        out_specs=[part, *(whole(rows) for rows in out_rows)],
        scratch_shapes=[
            pltpu.VMEM((seq, 2 * BLK), jnp.bfloat16),
            pltpu.VMEM((seq, R), jnp.float32),
            pltpu.VMEM((seq, R), jnp.float32),
            pltpu.VMEM((seq, 2 * BLK), jnp.float32),
            pltpu.VMEM((R, BLK), jnp.float32),
            pltpu.VMEM((R, BLK), jnp.bfloat16),
            pltpu.VMEM((R, BLK), jnp.bfloat16),
            *(pltpu.VMEM((LONG // 2 * KC, R), jnp.bfloat16) for _ in range(4)),
            pltpu.SMEM((seq // BLK // 2,), jnp.int32),
        ],
        out_shape=[
            jax.ShapeDtypeStruct((toks, width), jnp.bfloat16),
            *(jax.ShapeDtypeStruct((rows, 2 * BLK), jnp.bfloat16) for rows in out_rows),
        ],
        compiler_params=pltpu.CompilerParams(
            dimension_semantics=("arbitrary", "arbitrary"), vmem_limit_bytes=60 * 2**20
        ),
        cost_estimate=pl.CostEstimate(
            flops=40 * 10**9, bytes_accessed=8 * 2**20, transcendentals=2 * 10**7
        ),
    )(q, do, *pieces)


NZ, NX = 4, 4
NY, NH, NC = 4, 2, 2
CORE_PAIRS = [(i, i ^ 1) for i in range(NY * NH * NC)]


def along_x(array, step):
    pairs = [
        (z * NX + x, z * NX + (x + step) % NX) for z in range(NZ) for x in range(NX)
    ]
    return lax.ppermute(array, "ctx", pairs)


def along_z(array, step):
    pairs = [
        (z * NX + x, (z + step) % NZ * NX + x) for z in range(NZ) for x in range(NX)
    ]
    return lax.ppermute(array, "ctx", pairs)


def swap_x(array, bits):
    pairs = [(i, i ^ bits) for i in range(NZ * NX)]
    return lax.ppermute(array, "ctx", pairs)


def swap_z(array, bits):
    high, low_bits = bits // NZ, bits % NZ
    size = NZ * NX
    pairs = [
        (i * size + j, (i ^ high * NC) * size + (j ^ low_bits * NX))
        for i in range(NY * NH * NC)
        for j in range(size)
    ]
    return lax.ppermute(array, ("dp", "ctx"), pairs)


X_SWAPS = (1, 3)
Z_SWAPS = (1, 3, 7)


def swap_order(swaps):
    order = [0]
    for bits in reversed(swaps):
        order += [place ^ bits for place in order]
    return order


def along_y(array, step):
    rest = NH * NC
    pairs = [(i, (i + step * rest) % (NY * rest)) for i in range(NY * rest)]
    return lax.ppermute(array, "dp", pairs)


def tag_kernel(positions_ref, kv_ref, out_ref):
    toks = kv_ref.shape[0]
    out_ref[:toks, :] = kv_ref[...]
    first = (positions_ref[0] // BLK).astype(jnp.float32)
    out_ref[toks:, :] = jnp.full((TAG, kv_ref.shape[1]), first).astype(out_ref.dtype)


def tagged_tokens(positions, kv):
    toks, width = kv.shape
    return pl.pallas_call(
        tag_kernel,
        in_specs=[
            pl.BlockSpec(memory_space=pltpu.SMEM),
            pl.BlockSpec(memory_space=pltpu.VMEM),
        ],
        out_specs=pl.BlockSpec(memory_space=pltpu.VMEM),
        out_shape=jax.ShapeDtypeStruct((toks + TAG, width), kv.dtype),
    )(positions, kv)


def cut_kernel(at_ref, a_ref, out_ref):
    out_ref[...] = a_ref[...].T


def cut_features(features, at, start, count):
    toks, model = features.shape
    piece = model // (NY * NH)
    gs = pltpu.PrefetchScalarGridSpec(
        num_scalar_prefetch=1,
        grid=(count,),
        in_specs=[pl.BlockSpec((toks, piece), lambda i, at: (0, at[start + i]))],
        out_specs=pl.BlockSpec((piece, toks), lambda i, at: (i, 0)),
    )
    return pl.pallas_call(
        cut_kernel,
        grid_spec=gs,
        out_shape=jax.ShapeDtypeStruct((count * piece, toks), features.dtype),
        cost_estimate=pl.CostEstimate(
            flops=0, bytes_accessed=2**20 * count, transcendentals=0
        ),
    )(at, features)


def project_kernel(factor, at_ref, a_ref, b_ref, c_ref, d0_ref, d1_ref, g0, g1, g2, g3, out_ref):
    h = pl.program_id(0)
    far = jnp.where(h == 0, d0_ref[...], d1_ref[...])
    total = mm(a_ref[...], g0[...]) + mm(b_ref[...], g1[...])
    total = total + mm(c_ref[...], g2[...]) + mm(far, g3[...])
    total = (total * factor).astype(out_ref.dtype)
    rows = total.shape[0] // (NZ * NX)
    x_order, z_order = swap_order(X_SWAPS), swap_order(Z_SWAPS)
    x_rank = [0] * len(x_order)
    for rank, place in enumerate(x_order):
        x_rank[place] = rank
    z_rank = [0] * len(z_order)
    for rank, place in enumerate(z_order):
        z_rank[place] = rank

    def ranked(ranks, place):
        found = jnp.int32(0)
        for i, rank in enumerate(ranks):
            found = jnp.where(place == i, rank, found)
        return found

    x_to = [ranked(x_rank, x ^ at_ref[1]) for x in range(NX)]
    for z in range(NZ):
        z_to = ranked(z_rank, (h * NZ + z) ^ at_ref[0])
        for x in range(NX):
            src = (z * NX + x) * rows
            to = pl.multiple_of((x_to[x] * NH * NZ + z_to) * rows, rows)
            out_ref[pl.ds(to, rows), :] = total[src : src + rows, :]


def project(home, left, right, far_a, far_b, grads, at, which, factor):
    toks, width = grads[0].shape
    piece = home.shape[0] // (NH * NC)
    full = pl.BlockSpec((piece, toks), lambda i, at: (i * NC + at[2 + which], 0))
    half = pl.BlockSpec((piece, toks), lambda i, at: (at[2 + which], 0))
    grad = pl.BlockSpec(memory_space=pltpu.VMEM)
    gs = pltpu.PrefetchScalarGridSpec(
        num_scalar_prefetch=1,
        grid=(NH,),
        in_specs=[full, full, full, half, half] + [grad] * 4,
        out_specs=pl.BlockSpec((NH * piece, width), lambda i, at: (0, 0)),
    )
    return pl.pallas_call(
        functools.partial(project_kernel, factor),
        grid_spec=gs,
        out_shape=jax.ShapeDtypeStruct((NH * piece, width), jnp.bfloat16),
        cost_estimate=pl.CostEstimate(
            flops=2**30, bytes_accessed=3 * 2**20, transcendentals=0
        ),
    )(at, home, left, right, far_a, far_b, *grads)


def total_of(*parts):
    return sum(part.astype(jnp.float32) for part in parts)


def project_back(grads, weight):
    return lax.dot_general(
        grads, weight, (((1,), (1,)), ((), ())), preferred_element_type=jnp.float32
    ).astype(jnp.bfloat16)[None]


def body(layer_input, kv_weight, kv_stored, queries, grad_out, positions):
    low = jnp.bfloat16
    tok_rows = queries.shape[1]
    width = kv_weight.shape[1]
    ctx_size = lax.axis_size("ctx")
    data_size = lax.axis_size("dp")
    seq_rows = tok_rows * ctx_size
    data_at, ctx_at = lax.axis_index("dp"), lax.axis_index("ctx")
    y_at, far_at, core_at = data_at // (NH * NC), data_at // NC % NH, data_at % NC
    z_at, x_at = ctx_at // NX, ctx_at % NX

    tagged = tagged_tokens(positions, kv_stored[0])
    steps = ((1, 0), (1, 1), (2, 0), (3, 0), (3, 1), (2, 1), (0, 0), (0, 1))
    table = [(y_at + dy) % NY * NH + h for dy, h in steps]
    at = jnp.stack([far_at * NZ + z_at, x_at, 1 - core_at, core_at, *table]).astype(jnp.int32)
    plus = cut_features(layer_input[0], at, 4, 3)
    minus = cut_features(layer_input[0], at, 7, 3)
    home = cut_features(layer_input[0], at, 10, 2)

    column = [along_z(tagged, step) for step in range(1, NZ)]
    *column, plus = lax.optimization_barrier((*column, plus))
    near = jnp.concatenate([tagged, *column], axis=0)
    half = near.shape[0] // 2
    left, right = along_x(near, 1), along_x(near, -1)
    left, right, minus, home = lax.optimization_barrier((left, right, minus, home))
    far_a, far_b = along_x(left[:half], 1), along_x(right[half:], -1)

    query, plus, minus = lax.optimization_barrier((queries[0], plus, minus))
    from_left, from_right = along_y(plus, 1), along_y(minus, -1)

    query_grad, *sums = attention(
        query, grad_out[0], (near, left, right, far_a, far_b), seq_rows
    )
    from_left, from_right, *sums = lax.optimization_barrier((from_left, from_right, *sums))
    keep, plus, minus, plus_late, minus_late = sums
    full = home.shape[0]
    held, _ = lax.optimization_barrier((kv_weight, near))
    weight = lax.all_gather(held, "dp", axis=0, tiled=True)

    cut = plus_late.shape[0]
    feats_left, feats_right = from_left, from_right
    from_left, from_right = along_x(plus, 1), along_x(minus, -1)
    from_left, from_right, feats_a, feats_b = lax.optimization_barrier(
        (from_left, from_right, feats_left[full:], feats_right[full:])
    )
    feats_a, feats_b = along_y(feats_a, 1), along_y(feats_b, -1)
    plus_late = total_of(plus_late, from_left[:cut]).astype(low)
    minus_late = total_of(minus_late, from_right[cut:]).astype(low)
    late_left, late_right = along_x(plus_late, 1), along_x(minus_late, -1)
    early = total_of(keep[:cut], late_left, from_right[:cut]).astype(low)
    late = total_of(keep[cut:], from_left[cut:], late_right).astype(low)
    spans = [early[:tok_rows], early[tok_rows:], late[:tok_rows], late[tok_rows:]]
    spans = [spans[0], *(along_z(spans[step], -step) for step in range(1, NZ))]
    *spans, feats_a, feats_b = lax.optimization_barrier((*spans, feats_a, feats_b))
    owned = total_of(*spans).astype(low)

    grads = [along_y(owned, 1), along_y(owned, -1), along_y(owned, 2)]

    def terms_for(which):
        factor = 1.0 / math.sqrt(data_size * seq_rows)
        feats = (home, feats_left, feats_right, feats_a, feats_b)
        return project(*feats, (owned, *grads), at, which, factor)

    other = lax.ppermute(terms_for(0), "dp", CORE_PAIRS)
    terms, input_grad = total_of(terms_for(1), other), None
    for swap, swaps in ((swap_x, X_SWAPS), (swap_z, Z_SWAPS)):
        for bits in swaps:
            terms = terms.astype(low)
            cut = terms.shape[0] // 2
            came = swap(terms[cut:], bits)
            if input_grad is None:
                input_grad = project_back(owned, weight)
                came, input_grad = lax.optimization_barrier((came, input_grad))
            terms = total_of(terms[:cut], came)
    weight_grad = terms

    return (query_grad[None], input_grad, weight_grad)


def solution(mesh):
    placed = (
        P("dp", "ctx", None),
        P("dp", None),
        P("dp", "ctx", None),
        P("dp", "ctx", None),
        P("dp", "ctx", None),
        P("ctx"),
    )
    return jax.shard_map(
        body,
        mesh=mesh,
        in_specs=placed,
        out_specs=(P("dp", "ctx", None), P("dp", "ctx", None), P(("dp", "ctx"), None)),
        check_vma=False,
    )
```

```python
import functools
import math

import jax
import jax.numpy as jnp
from jax import lax
from jax.experimental import pallas as pl
from jax.experimental.pallas import tpu as pltpu
from jax.sharding import PartitionSpec as P

BLK = 128
TAG = 16
MASKED = -1e30
LONG = 4


def mm(a, b):
    return lax.dot_general(a, b, (((1,), (0,)), ((), ())), preferred_element_type=jnp.float32)


def mm_tn(a, b):
    return lax.dot_general(a, b, (((0,), (0,)), ((), ())), preferred_element_type=jnp.float32)


def mm_nt(a, b):
    return lax.dot_general(a, b, (((1,), (1,)), ((), ())), preferred_element_type=jnp.float32)


def attn_kernel(
    G,
    KC,
    blocks,
    scale,
    q_ref,
    do_ref,
    near_ref,
    left_ref,
    right_ref,
    far_a_ref,
    far_b_ref,
    dq_ref,
    keep_ref,
    plus_ref,
    minus_ref,
    plus_late_ref,
    minus_late_ref,
    kvs,
    s_scr,
    dp_scr,
    acc,
    dq_acc,
    qr,
    dor,
    p_even,
    d_even,
    p_odd,
    d_odd,
    first_ref,
):
    R = G * BLK
    c = scale * math.log2(math.e)
    side = pl.program_id(0)
    grp = pl.program_id(1)
    toks = 2 * BLK
    owners = blocks // 2

    @pl.when((side == 0) & (grp == 0))
    def _():
        acc[...] = jnp.zeros_like(acc)
        owner = 0
        for piece in (near_ref, left_ref, right_ref, far_a_ref, far_b_ref):
            for i in range(piece.shape[0] // (toks + TAG)):
                base = i * (toks + TAG)
                mark = piece[base + toks : base + toks + TAG, :BLK].astype(jnp.float32)
                first = jnp.max(mark).astype(jnp.int32)
                first_ref[owner] = first
                for half, place in ((0, first), (1, blocks - 1 - first)):
                    dst = pl.ds(pl.multiple_of(place * BLK, BLK), BLK)
                    kvs[dst, :] = piece[base + half * BLK : base + (half + 1) * BLK, :]
                owner += 1

    for h in range(G):
        cols = slice(h * BLK, (h + 1) * BLK)
        qr[cols, :] = q_ref[:, cols]
        dor[cols, :] = do_ref[:, cols]
    dq_acc[...] = jnp.zeros_like(dq_acc)
    qb = jnp.where(side == 0, first_ref[0], blocks - 1 - first_ref[0])
    nk = (qb + KC // BLK) // (KC // BLK)

    def scores(start, size, state, masked):
        m, l, d = state
        rows = pl.ds(pl.multiple_of(start, KC), size)
        s = mm_nt(kvs[rows, :BLK], qr[...])
        dp = mm_nt(kvs[rows, BLK:], dor[...])
        if masked:
            kpos = start + lax.broadcasted_iota(jnp.int32, (size, R), 0)
            qpos = qb * BLK + (lax.broadcasted_iota(jnp.int32, (size, R), 1) & (BLK - 1))
            s = jnp.where(kpos <= qpos, s, MASKED)
        s_scr[rows, :] = s
        dp_scr[rows, :] = dp
        s3 = s.reshape(size // 8, 8, R)
        new = jnp.maximum(m, jnp.max(s3, axis=0))
        p = jnp.exp2((s3 - new[None]) * c)
        f = jnp.exp2((m - new) * c)
        l = l * f + jnp.sum(p, axis=0)
        d = d * f + jnp.sum(p * dp.reshape(size // 8, 8, R), axis=0)
        return new, l, d

    state = (
        jnp.full((8, R), MASKED, jnp.float32),
        jnp.zeros((8, R), jnp.float32),
        jnp.zeros((8, R), jnp.float32),
    )
    runs = (nk - 1) // LONG
    state = lax.fori_loop(
        0, runs, lambda i, state: scores(i * LONG * KC, LONG * KC, state, False), state
    )
    done = runs * LONG
    middle = (nk - 1 - done) // 2
    state = lax.fori_loop(
        0, middle, lambda i, state: scores(done * KC, 2 * KC, state, False), state
    )
    state = lax.fori_loop(
        done + 2 * middle, nk - 1, lambda i, state: scores(i * KC, KC, state, False), state
    )
    m, l, d = scores((nk - 1) * KC, KC, state, True)
    top = jnp.max(m, axis=0, keepdims=True)
    f = jnp.exp2((m - top) * c)
    total = jnp.sum(l * f, axis=0, keepdims=True)
    dvec = jnp.sum(d * f, axis=0, keepdims=True) / total
    lse = top * c + jnp.log2(total)

    def weigh(start, size, p_buf, d_buf):
        rows = pl.ds(pl.multiple_of(start, KC), size)
        p = jnp.exp2(s_scr[rows, :] * c - lse)
        d_buf[:size, :] = (p * (dp_scr[rows, :] - dvec)).astype(jnp.bfloat16)
        p_buf[:size, :] = p.astype(jnp.bfloat16)

    def spend(start, size, p_buf, d_buf):
        rows = pl.ds(pl.multiple_of(start, KC), size)
        dq_acc[...] += mm_tn(d_buf[:size, :], kvs[rows, :BLK])
        acc[rows, :BLK] += mm(d_buf[:size, :], qr[...])
        acc[rows, BLK:] += mm(p_buf[:size, :], dor[...])

    run = p_even.shape[0]
    pairs = nk // (2 * run // KC)

    @pl.when(pairs > 0)
    def _():
        weigh(0, run, p_even, d_even)

    def pair(i, _):
        start = i * 2 * run
        weigh(start + run, run, p_odd, d_odd)
        spend(start, run, p_even, d_even)
        weigh(jnp.minimum(start + 2 * run, blocks * BLK - run), run, p_even, d_even)
        spend(start + run, run, p_odd, d_odd)
        return 0

    def single(i, _):
        weigh(i * KC, KC, p_even, d_even)
        spend(i * KC, KC, p_even, d_even)
        return 0

    lax.fori_loop(0, pairs, pair, 0)
    spent = pairs * (2 * run // KC)
    left = (nk - spent) // (run // KC)

    @pl.when(left > 0)
    def _():
        weigh(spent * KC, run, p_even, d_even)
        spend(spent * KC, run, p_even, d_even)

    lax.fori_loop(spent + left * (run // KC), nk, single, 0)

    for h in range(G):
        cols = slice(h * BLK, (h + 1) * BLK)
        dq_ref[:, cols] = (dq_acc[cols, :] * scale).astype(jnp.bfloat16)

    @pl.when((side == pl.num_programs(0) - 1) & (grp == pl.num_programs(1) - 1))
    def _():
        span = owners // NX
        cut = span // 2
        for owner in range(owners):
            dx, dz = owner // span, owner % span
            late = dz >= cut
            if dx == 0:
                out, row = keep_ref, dz
            elif dx == 1:
                out, row = (minus_late_ref, dz - cut) if late else (minus_ref, dz)
            elif dx == 2:
                out, row = (plus_ref, dz) if late else (plus_late_ref, dz)
            else:
                out, row = (minus_ref, dz) if late else (plus_ref, dz)
            first = first_ref[owner]
            for half, place in ((0, first), (1, blocks - 1 - first)):
                src = pl.ds(pl.multiple_of(place * BLK, BLK), BLK)
                dst = slice(row * toks + half * BLK, row * toks + (half + 1) * BLK)
                out[dst, :BLK] = (acc[src, :BLK] * scale).astype(jnp.bfloat16)
                out[dst, BLK:] = acc[src, BLK:].astype(jnp.bfloat16)


def attention(q, do, pieces, seq, G=8, KC=256):
    toks, width = q.shape
    heads = width // BLK
    R = G * BLK
    part = pl.BlockSpec((BLK, R), lambda s, g: (s, g))
    quarter = seq // NX

    def whole(rows):
        return pl.BlockSpec((rows, 2 * BLK), lambda s, g: (0, 0), pipeline_mode=pl.Buffered(1))

    out_rows = (quarter, quarter, quarter, quarter // 2, quarter // 2)
    return pl.pallas_call(
        functools.partial(attn_kernel, G, KC, seq // BLK, 1.0 / math.sqrt(BLK)),
        grid=(2, heads // G),
        in_specs=[part, part, *(whole(piece.shape[0]) for piece in pieces)],
        out_specs=[part, *(whole(rows) for rows in out_rows)],
        scratch_shapes=[
            pltpu.VMEM((seq, 2 * BLK), jnp.bfloat16),
            pltpu.VMEM((seq, R), jnp.float32),
            pltpu.VMEM((seq, R), jnp.float32),
            pltpu.VMEM((seq, 2 * BLK), jnp.float32),
            pltpu.VMEM((R, BLK), jnp.float32),
            pltpu.VMEM((R, BLK), jnp.bfloat16),
            pltpu.VMEM((R, BLK), jnp.bfloat16),
            *(pltpu.VMEM((LONG // 2 * KC, R), jnp.bfloat16) for _ in range(4)),
            pltpu.SMEM((seq // BLK // 2,), jnp.int32),
        ],
        out_shape=[
            jax.ShapeDtypeStruct((toks, width), jnp.bfloat16),
            *(jax.ShapeDtypeStruct((rows, 2 * BLK), jnp.bfloat16) for rows in out_rows),
        ],
        compiler_params=pltpu.CompilerParams(
            dimension_semantics=("arbitrary", "arbitrary"), vmem_limit_bytes=60 * 2**20
        ),
        cost_estimate=pl.CostEstimate(
            flops=40 * 10**9, bytes_accessed=8 * 2**20, transcendentals=2 * 10**7
        ),
    )(q, do, *pieces)


NZ, NX = 4, 4
NY, NH, NC = 4, 2, 2
CORE_PAIRS = [(i, i ^ 1) for i in range(NY * NH * NC)]


def along_x(array, step):
    pairs = [
        (z * NX + x, z * NX + (x + step) % NX) for z in range(NZ) for x in range(NX)
    ]
    return lax.ppermute(array, "ctx", pairs)


def along_z(array, step):
    pairs = [
        (z * NX + x, (z + step) % NZ * NX + x) for z in range(NZ) for x in range(NX)
    ]
    return lax.ppermute(array, "ctx", pairs)


def swap_x(array, bits):
    pairs = [(i, i ^ bits) for i in range(NZ * NX)]
    return lax.ppermute(array, "ctx", pairs)


def swap_z(array, bits):
    high, low_bits = bits // NZ, bits % NZ
    size = NZ * NX
    pairs = [
        (i * size + j, (i ^ high * NC) * size + (j ^ low_bits * NX))
        for i in range(NY * NH * NC)
        for j in range(size)
    ]
    return lax.ppermute(array, ("dp", "ctx"), pairs)


X_SWAPS = (1, 3)
Z_SWAPS = (1, 3, 7)


def swap_order(swaps):
    order = [0]
    for bits in reversed(swaps):
        order += [place ^ bits for place in order]
    return order


def along_y(array, step):
    rest = NH * NC
    pairs = [(i, (i + step * rest) % (NY * rest)) for i in range(NY * rest)]
    return lax.ppermute(array, "dp", pairs)


def tag_kernel(positions_ref, kv_ref, out_ref):
    toks = kv_ref.shape[0]
    out_ref[:toks, :] = kv_ref[...]
    first = (positions_ref[0] // BLK).astype(jnp.float32)
    out_ref[toks:, :] = jnp.full((TAG, kv_ref.shape[1]), first).astype(out_ref.dtype)


def tagged_tokens(positions, kv):
    toks, width = kv.shape
    return pl.pallas_call(
        tag_kernel,
        in_specs=[
            pl.BlockSpec(memory_space=pltpu.SMEM),
            pl.BlockSpec(memory_space=pltpu.VMEM),
        ],
        out_specs=pl.BlockSpec(memory_space=pltpu.VMEM),
        out_shape=jax.ShapeDtypeStruct((toks + TAG, width), kv.dtype),
    )(positions, kv)


def cut_kernel(at_ref, a_ref, out_ref):
    out_ref[...] = a_ref[...].T


def cut_features(features, at, start, count):
    toks, model = features.shape
    piece = model // (NY * NH)
    gs = pltpu.PrefetchScalarGridSpec(
        num_scalar_prefetch=1,
        grid=(count,),
        in_specs=[pl.BlockSpec((toks, piece), lambda i, at: (0, at[start + i]))],
        out_specs=pl.BlockSpec((piece, toks), lambda i, at: (i, 0)),
    )
    return pl.pallas_call(
        cut_kernel,
        grid_spec=gs,
        out_shape=jax.ShapeDtypeStruct((count * piece, toks), features.dtype),
        cost_estimate=pl.CostEstimate(
            flops=0, bytes_accessed=2**20 * count, transcendentals=0
        ),
    )(at, features)


def project_kernel(factor, at_ref, a_ref, b_ref, c_ref, d0_ref, d1_ref, g0, g1, g2, g3, out_ref):
    h = pl.program_id(0)
    far = jnp.where(h == 0, d0_ref[...], d1_ref[...])
    total = mm(a_ref[...], g0[...]) + mm(b_ref[...], g1[...])
    total = total + mm(c_ref[...], g2[...]) + mm(far, g3[...])
    total = (total * factor).astype(out_ref.dtype)
    rows = total.shape[0] // (NZ * NX)
    x_order, z_order = swap_order(X_SWAPS), swap_order(Z_SWAPS)
    x_rank = [0] * len(x_order)
    for rank, place in enumerate(x_order):
        x_rank[place] = rank
    z_rank = [0] * len(z_order)
    for rank, place in enumerate(z_order):
        z_rank[place] = rank

    def ranked(ranks, place):
        found = jnp.int32(0)
        for i, rank in enumerate(ranks):
            found = jnp.where(place == i, rank, found)
        return found

    x_to = [ranked(x_rank, x ^ at_ref[1]) for x in range(NX)]
    for z in range(NZ):
        z_to = ranked(z_rank, (h * NZ + z) ^ at_ref[0])
        for x in range(NX):
            src = (z * NX + x) * rows
            to = pl.multiple_of((x_to[x] * NH * NZ + z_to) * rows, rows)
            out_ref[pl.ds(to, rows), :] = total[src : src + rows, :]


def project(home, left, right, far_a, far_b, grads, at, which, factor):
    toks, width = grads[0].shape
    piece = home.shape[0] // (NH * NC)
    full = pl.BlockSpec((piece, toks), lambda i, at: (i * NC + at[2 + which], 0))
    half = pl.BlockSpec((piece, toks), lambda i, at: (at[2 + which], 0))
    grad = pl.BlockSpec(memory_space=pltpu.VMEM)
    gs = pltpu.PrefetchScalarGridSpec(
        num_scalar_prefetch=1,
        grid=(NH,),
        in_specs=[full, full, full, half, half] + [grad] * 4,
        out_specs=pl.BlockSpec((NH * piece, width), lambda i, at: (0, 0)),
    )
    return pl.pallas_call(
        functools.partial(project_kernel, factor),
        grid_spec=gs,
        out_shape=jax.ShapeDtypeStruct((NH * piece, width), jnp.bfloat16),
        cost_estimate=pl.CostEstimate(
            flops=2**30, bytes_accessed=3 * 2**20, transcendentals=0
        ),
    )(at, home, left, right, far_a, far_b, *grads)


def total_of(*parts):
    return sum(part.astype(jnp.float32) for part in parts)


def project_back(grads, weight):
    return lax.dot_general(
        grads, weight, (((1,), (1,)), ((), ())), preferred_element_type=jnp.float32
    ).astype(jnp.bfloat16)[None]


def body(layer_input, kv_weight, kv_stored, queries, grad_out, positions):
    low = jnp.bfloat16
    tok_rows = queries.shape[1]
    width = kv_weight.shape[1]
    ctx_size = lax.axis_size("ctx")
    data_size = lax.axis_size("dp")
    seq_rows = tok_rows * ctx_size
    data_at, ctx_at = lax.axis_index("dp"), lax.axis_index("ctx")
    y_at, far_at, core_at = data_at // (NH * NC), data_at // NC % NH, data_at % NC
    z_at, x_at = ctx_at // NX, ctx_at % NX

    tagged = tagged_tokens(positions, kv_stored[0])
    steps = ((1, 0), (1, 1), (2, 0), (3, 0), (3, 1), (2, 1), (0, 0), (0, 1))
    table = [(y_at + dy) % NY * NH + h for dy, h in steps]
    at = jnp.stack([far_at * NZ + z_at, x_at, 1 - core_at, core_at, *table]).astype(jnp.int32)
    plus = cut_features(layer_input[0], at, 4, 3)
    minus = cut_features(layer_input[0], at, 7, 3)
    home = cut_features(layer_input[0], at, 10, 2)

    column = [along_z(tagged, step) for step in range(1, NZ)]
    *column, plus = lax.optimization_barrier((*column, plus))
    near = jnp.concatenate([tagged, *column], axis=0)
    half = near.shape[0] // 2
    left, right = along_x(near, 1), along_x(near, -1)
    left, right, minus, home = lax.optimization_barrier((left, right, minus, home))
    far_a, far_b = along_x(left[:half], 1), along_x(right[half:], -1)

    query, plus, minus = lax.optimization_barrier((queries[0], plus, minus))
    from_left, from_right = along_y(plus, 1), along_y(minus, -1)

    query_grad, *sums = attention(
        query, grad_out[0], (near, left, right, far_a, far_b), seq_rows
    )
    from_left, from_right, *sums = lax.optimization_barrier((from_left, from_right, *sums))
    keep, plus, minus, plus_late, minus_late = sums
    full = home.shape[0]
    held, _ = lax.optimization_barrier((kv_weight, near))
    weight = lax.all_gather(held, "dp", axis=0, tiled=True)

    cut = plus_late.shape[0]
    feats_left, feats_right = from_left, from_right
    from_left, from_right = along_x(plus, 1), along_x(minus, -1)
    from_left, from_right, feats_a, feats_b = lax.optimization_barrier(
        (from_left, from_right, feats_left[full:], feats_right[full:])
    )
    feats_a, feats_b = along_y(feats_a, 1), along_y(feats_b, -1)
    plus_late = total_of(plus_late, from_left[:cut]).astype(low)
    minus_late = total_of(minus_late, from_right[cut:]).astype(low)
    late_left, late_right = along_x(plus_late, 1), along_x(minus_late, -1)
    early = total_of(keep[:cut], late_left, from_right[:cut]).astype(low)
    late = total_of(keep[cut:], from_left[cut:], late_right).astype(low)
    spans = [early[:tok_rows], early[tok_rows:], late[:tok_rows], late[tok_rows:]]
    spans = [spans[0], *(along_z(spans[step], -step) for step in range(1, NZ))]
    *spans, feats_a, feats_b = lax.optimization_barrier((*spans, feats_a, feats_b))
    owned = total_of(*spans).astype(low)

    grads = [along_y(owned, 1), along_y(owned, -1), along_y(owned, 2)]

    def terms_for(which):
        factor = 1.0 / math.sqrt(data_size * seq_rows)
        feats = (home, feats_left, feats_right, feats_a, feats_b)
        return project(*feats, (owned, *grads), at, which, factor)

    other = lax.ppermute(terms_for(0), "dp", CORE_PAIRS)
    terms, input_grad = total_of(terms_for(1), other), None
    for swap, swaps in ((swap_x, X_SWAPS), (swap_z, Z_SWAPS)):
        for bits in swaps:
            terms = terms.astype(low)
            cut = terms.shape[0] // 2
            came = swap(terms[cut:], bits)
            if input_grad is None:
                input_grad = project_back(owned, weight)
                came, input_grad = lax.optimization_barrier((came, input_grad))
            terms = total_of(terms[:cut], came)
    weight_grad = terms

    return (query_grad[None], input_grad, weight_grad)


def solution(mesh):
    placed = (
        P("dp", "ctx", None),
        P("dp", None),
        P("dp", "ctx", None),
        P("dp", "ctx", None),
        P("dp", "ctx", None),
        P("ctx"),
    )
    return jax.shard_map(
        body,
        mesh=mesh,
        in_specs=placed,
        out_specs=(P("dp", "ctx", None), P("dp", "ctx", None), P(("dp", "ctx"), None)),
        check_vma=False,
    )
```
